512 devices in a mesh: blk: 16 (over z_hi, x, core), grp: 32 (over y, z_lo).
Axes of the slice: x: 4, y: 4, z: 16 (z_hi: 2, z_lo: 8; z = z_hi * 8 + z_lo), core: 2. Of those that a mesh axis runs over, the one named last changes fastest.
Arguments:
- picture_vectors: bfloat16 [98304, 640], P(('blk', 'grp')), may hold values from -0.23925781 to 0.23925781
- caption_vectors: bfloat16 [98304, 640], P(('blk', 'grp')), may hold values from -0.23925781 to 0.23925781
- picture_match_label: int32 [98304], P(('blk', 'grp')), may hold values from 0 to 255
- caption_match_label: int32 [98304], P(('blk', 'grp')), may hold values from 0 to 255
- inverse_softness: float32 [1], replicated, may hold values from 6 to 16
- score_offset: float32 [1], replicated, may hold values from -3 to -1
Outputs:
- image_grad: bfloat16 [98304, 640], P(('blk', 'grp'))
- text_grad: float32 [98304, 640], P(('blk', 'grp'))
The draws below stay inside these ranges and needn't reach their ends.
Inputs may be any that keep to these rules, and one draw needn't show every extreme that they name: `picture_match_label`: pair ids; an image and a text form a positive pair when their ids are equal. `caption_match_label`: pair ids, as for the images.
All inputs are finite; a program needn't handle non-finite values.
Results may differ from the reference program's by a relative error of at most 0.0034.
Values may be sent and summed in bfloat16 or wider, within the bound.
No kernel may reach another device: no remote copies, remote signals or barrier semaphores. Data moves between devices by JAX's collectives and lax.ppermute only.
A program may use at most 64 MiB of HBM per device.

```python
import math
import jax
import jax.numpy as jnp
from jax import lax

D = 640
PAIR_COUNT = 256
ROWS_PER_BLOCK = 6144
IMAGES = 98304
TEXTS = 98304
N_BLK = 16


def plant(values, rng, smallest, largest):
    extent = values.shape
    spot = [jax.random.randint(jax.random.fold_in(rng, axis), (), 0, extent[axis]) for axis in range(len(extent))]
    values = values.at[tuple(spot)].set(smallest)
    longest = extent.index(max(extent))
    spot[longest] = (spot[longest] + 1) % extent[longest]
    return values.at[tuple(spot)].set(largest)


def shard_levels(rng, extent, shards, smallest, top_value):
    def one(position, parts):
        draws = jax.random.uniform(jax.random.fold_in(jax.random.fold_in(rng, 6), position), (parts,), jnp.float32, smallest / len(shards), top_value / len(shards))
        return jnp.repeat(jnp.exp(draws), extent[position] // parts).reshape((-1,) + (1,) * (len(extent) - position - 1))

    gain = one(*shards[0])
    for cut in shards[1:]:
        gain = gain * one(*cut)
    return gain


def bell_draw(own_key, extent, deviation, reach, cuts=(), kind=jnp.bfloat16):
    values = jax.random.normal(own_key, extent, jnp.float32) * deviation
    if len(cuts) > 0:
        values = shard_levels(own_key, extent, cuts, -0.22, 0.18) * values
    return jnp.clip(values, min=-reach, max=reach).astype(kind)


def setup_inputs(seed: int = 0) -> dict:
    streams_of = jax.random.split(jax.random.key(seed), 7)
    picture_vectors = bell_draw(streams_of[0], (IMAGES, D), 0.04, 0.23925781, ((0, 512),))
    caption_vectors = bell_draw(streams_of[1], (TEXTS, D), 0.04, 0.23925781, ((0, 512),))
    picture_match_label = plant(jax.random.randint(streams_of[2], (IMAGES,), 0, PAIR_COUNT), jax.random.fold_in(streams_of[2], 1), 0, PAIR_COUNT - 1).astype(jnp.int32)
    caption_match_label = plant(jax.random.randint(streams_of[3], (TEXTS,), 0, PAIR_COUNT), jax.random.fold_in(streams_of[3], 1), 0, PAIR_COUNT - 1).astype(jnp.int32)
    inverse_softness = jnp.clip(jnp.exp(jax.random.uniform(streams_of[4], (1,), jnp.float32, math.log(6.0), math.log(16.0))), 6.0, 16.0)
    score_offset = jnp.clip(jax.random.uniform(streams_of[5], (1,), jnp.float32, -3.0, -1.0), -3.0, -1.0)
    return dict(picture_vectors=picture_vectors, caption_vectors=caption_vectors, picture_match_label=picture_match_label, caption_match_label=caption_match_label, inverse_softness=inverse_softness, score_offset=score_offset)


def reference(picture_vectors, caption_vectors, picture_match_label, caption_match_label, inverse_softness, score_offset):
    rows = ROWS_PER_BLOCK
    score_factor = inverse_softness[0]
    logit_bias = score_offset[0]

    def one_block(block):
        start = (block * rows).astype(jnp.int32)
        images_of_block = lax.dynamic_slice_in_dim(picture_vectors, start, rows, 0)
        block_ids = lax.dynamic_slice_in_dim(picture_match_label, start, rows, 0)
        other = ((block + N_BLK - 1) % N_BLK).astype(jnp.int32)
        text_start = (other * rows).astype(jnp.int32)
        block_texts = lax.dynamic_slice_in_dim(caption_vectors, text_start, rows, 0)
        block_tids = lax.dynamic_slice_in_dim(caption_match_label, text_start, rows, 0)
        scores = jnp.dot(images_of_block, block_texts.T, preferred_element_type=jnp.float32) * score_factor + logit_bias
        positive = (block_ids[:, None] == block_tids[None, :]).astype(jnp.float32)
        weight = ((jax.nn.sigmoid(scores) - positive) / 8.0).astype(jnp.bfloat16)
        image_portion = (score_factor * jnp.dot(weight, block_texts, preferred_element_type=jnp.float32)).astype(jnp.bfloat16)
        text_part = score_factor * jnp.dot(weight.T, images_of_block, preferred_element_type=jnp.float32)
        return image_portion, text_part

    image_blocks, text_blocks = lax.map(one_block, jnp.arange(N_BLK, dtype=jnp.int32))
    text_blocks = jnp.roll(text_blocks, -1, axis=0)
    return image_blocks.reshape(IMAGES, D), text_blocks.reshape(TEXTS, D)
```

```python
import itertools

import jax
import jax.numpy as jnp
import numpy as np
from jax import lax
from jax.experimental import pallas as pl
from jax.experimental.pallas import tpu as pltpu
from jax.sharding import Mesh, PartitionSpec as P

AXES = ("h", "x", "c", "y", "z")
SIZES = dict(h=2, x=4, c=2, y=4, z=8)
MOVE_AXES = ("h", "x", "c", "z")
ROWS = 192
EXTRA = 16
PACKED = ROWS + EXTRA
D = 640
GROUP = 4 * ROWS
CHUNK = 256

PLANE = (7, 3, 0, 5, 2, 6, 1, 4)
IMAGE_PLACE = ((0, 3, 5, 6, 4, 7, 2, 1), (6, 7, 0, 1, 3, 4, 2, 5), (1, 0, 5, 3, 6, 7, 2, 4), (1, 5, 3, 6, 2, 7, 4, 0), (4, 2, 0, 3, 6, 1, 5, 7), (6, 2, 7, 0, 3, 5, 1, 4), (7, 1, 6, 5, 4, 3, 0, 2), (6, 5, 4, 3, 2, 0, 7, 1))
TEXT_PLACE = ((3, 2, 4, 1, 6, 0, 7, 5), (3, 7, 4, 6, 2, 5, 1, 0), (5, 4, 6, 1, 0, 2, 3, 7), (5, 2, 0, 1, 7, 4, 6, 3), (3, 7, 0, 4, 1, 2, 5, 6), (0, 3, 4, 7, 1, 5, 2, 6), (6, 2, 5, 3, 1, 4, 0, 7), (6, 1, 2, 4, 0, 7, 5, 3))


def routes(place, shift):
    extent = tuple(SIZES[a] for a in MOVE_AXES)
    out = []
    for h, x, c, z in itertools.product(*map(range, extent)):
        pair = (8 * h + 2 * x + c + shift) % 16
        half, p = divmod(pair, 8)
        spot = place[p][z]
        to = (half, spot // 2, spot % 2, PLANE[p])
        out.append((int(np.ravel_multi_index((h, x, c, z), extent)), int(np.ravel_multi_index(to, extent))))
    return out


IMAGE_ROUTE = routes(IMAGE_PLACE, 0)
TEXT_ROUTE = routes(TEXT_PLACE, 1)


def back(route):
    return [(b, a) for a, b in route]


def pack(rows, ids, slot):
    flat = lax.dynamic_update_slice(jnp.zeros((EXTRA * D,), jnp.bfloat16), ids.astype(jnp.bfloat16), (slot * ROWS,))
    return jnp.concatenate([rows, flat.reshape(EXTRA, D)], axis=0)


def id_row(ref):
    parts = ref[0, ROWS:, :].astype(jnp.float32)
    for k in range(1, 4):
        parts = parts + ref[k, ROWS:, :].astype(jnp.float32)
    return jnp.concatenate([parts[0:1, :], parts[1:2, : GROUP - D]], axis=1)


def pair_kernel(scale_ref, own_ref, other_ref, text_ref, own_grad_ref, other_grad_ref, text_grad_ref, images, texts, weights, id_columns, sums):
    factor = scale_ref[0]
    offset = scale_ref[1]
    out_factor = factor * 0.125
    for k in range(4):
        texts[k * ROWS : (k + 1) * ROWS, :] = text_ref[k, :ROWS, :]
        images[k * ROWS : (k + 1) * ROWS, :] = own_ref[k, :ROWS, :]
        images[GROUP + k * ROWS : GROUP + (k + 1) * ROWS, :] = other_ref[k, :ROWS, :]
    text_ids = id_row(text_ref)
    for half, ref in enumerate((own_ref, other_ref)):
        ids = id_row(ref)
        for j in range(GROUP // 128):
            tile = jnp.broadcast_to(ids[:, j * 128 : (j + 1) * 128], (128, 128))
            id_columns[half * GROUP + j * 128 : half * GROUP + (j + 1) * 128, :] = tile.T

    def step(i, _):
        start = pl.multiple_of(i * CHUNK, CHUNK)
        block = images[pl.ds(start, CHUNK), :]
        scores = lax.dot_general(block, texts[...], (((1,), (1,)), ((), ())), preferred_element_type=jnp.float32)
        scores = scores * factor + offset
        columns = id_columns[pl.ds(start, CHUNK), :]
        positive = (jnp.concatenate([columns] * (GROUP // 128), axis=1) == text_ids).astype(jnp.float32)
        weight = (jax.nn.sigmoid(scores) - positive).astype(jnp.bfloat16)
        weights[pl.ds(start, CHUNK), :] = weight
        sums[pl.ds(start, CHUNK), :] = out_factor * jnp.dot(weight, texts[...], preferred_element_type=jnp.float32)
        return 0

    lax.fori_loop(0, 2 * GROUP // CHUNK, step, 0)
    for k in range(4):
        own_grad_ref[k] = sums[k * ROWS : (k + 1) * ROWS, :].astype(own_grad_ref.dtype)
        other_grad_ref[k] = sums[GROUP + k * ROWS : GROUP + (k + 1) * ROWS, :].astype(other_grad_ref.dtype)

    def text_step(j, _):
        start = pl.multiple_of(j * CHUNK, CHUNK)
        sums[pl.ds(start, CHUNK), :] = out_factor * lax.dot_general(
            weights[:, pl.ds(start, CHUNK)], images[...], (((0,), (0,)), ((), ())), preferred_element_type=jnp.float32
        )
        return 0

    for j in range(GROUP // CHUNK):
        text_step(j, 0)
    for k in range(4):
        text_grad_ref[k] = sums[k * ROWS : (k + 1) * ROWS, :].astype(text_grad_ref.dtype)


def pair_grads(scale, own, other, text):
    vmem = pl.BlockSpec(memory_space=pltpu.VMEM)
    grad = lambda kind: jax.ShapeDtypeStruct((4, ROWS, D), kind)
    return pl.pallas_call(
        pair_kernel,
        out_shape=(grad(jnp.float32), grad(jnp.bfloat16), grad(jnp.bfloat16)),
        in_specs=[pl.BlockSpec(memory_space=pltpu.SMEM), vmem, vmem, vmem],
        out_specs=(vmem, vmem, vmem),
        scratch_shapes=[
            pltpu.VMEM((2 * GROUP, D), jnp.bfloat16),
            pltpu.VMEM((GROUP, D), jnp.bfloat16),
            pltpu.VMEM((2 * GROUP, GROUP), jnp.bfloat16),
            pltpu.VMEM((2 * GROUP, 128), jnp.float32),
            pltpu.VMEM((2 * GROUP, D), jnp.float32),
        ],
        compiler_params=pltpu.CompilerParams(vmem_limit_bytes=48 * 1024 * 1024),
        cost_estimate=pl.CostEstimate(flops=6 * 2 * GROUP * GROUP * D, bytes_accessed=10 << 20, transcendentals=2 * GROUP * GROUP),
        name="pair_grads",
    )(scale, own, other, text)


def body(picture_vectors, caption_vectors, picture_match_label, caption_match_label, inverse_softness, score_offset):
    scale = jnp.concatenate([inverse_softness, score_offset])
    place = jnp.asarray(np.asarray(IMAGE_PLACE, np.int32))
    image_slot = place[2 * lax.axis_index("x") + lax.axis_index("c"), lax.axis_index("z")] // 2
    packed_images = pack(picture_vectors, picture_match_label, image_slot)
    packed_texts = pack(caption_vectors, caption_match_label, lax.axis_index("y"))
    images = lax.ppermute(packed_images, MOVE_AXES, IMAGE_ROUTE)
    texts = lax.ppermute(packed_texts, MOVE_AXES, TEXT_ROUTE)
    own = lax.all_gather(images, "x", axis=0)
    other = lax.ppermute(own, "c", [(0, 1), (1, 0)])
    text = lax.all_gather(texts, "y", axis=0)
    own_grad, other_grad, text_part = pair_grads(scale, own, other, text)
    other_grad = lax.ppermute(other_grad, "c", [(0, 1), (1, 0)])
    image_part = (own_grad + other_grad.astype(jnp.float32)).astype(jnp.bfloat16)
    text_parts = lax.all_to_all(text_part, "y", split_axis=0, concat_axis=0, tiled=True)
    text_sum = jnp.sum(text_parts.astype(jnp.float32), axis=0).astype(jnp.bfloat16)
    text_home = lax.ppermute(text_sum, MOVE_AXES, back(TEXT_ROUTE))
    image_parts = lax.all_to_all(image_part, "x", split_axis=0, concat_axis=0, tiled=True)
    image_sum = jnp.sum(image_parts.astype(jnp.float32), axis=0).astype(jnp.bfloat16)
    image_home = lax.ppermute(image_sum, MOVE_AXES, back(IMAGE_ROUTE))
    return image_home, text_home.astype(jnp.float32)


def solution(mesh):
    fine = Mesh(mesh.devices.reshape(tuple(SIZES.values())), AXES)
    rows, ids = P(AXES, None), P(AXES)
    return jax.shard_map(
        body,
        mesh=fine,
        in_specs=(rows, rows, ids, ids, P(), P()),
        out_specs=(rows, rows),
        check_vma=False,
    )
```

```python
import itertools

import jax
import jax.numpy as jnp
import numpy as np
from jax import lax
from jax.experimental import pallas as pl
from jax.experimental.pallas import tpu as pltpu
from jax.sharding import Mesh, PartitionSpec as P

AXES = ("h", "x", "c", "y", "z")
SIZES = dict(h=2, x=4, c=2, y=4, z=8)
MOVE_AXES = ("h", "x", "c", "z")
ROWS = 192
EXTRA = 8
PACKED = ROWS + EXTRA
D = 640
GROUP = 4 * ROWS
CHUNK = 256

PLANE = (7, 3, 0, 5, 2, 6, 1, 4)
IMAGE_PLACE = ((0, 2, 4, 6, 1, 3, 5, 7), (0, 2, 4, 6, 1, 3, 5, 7), (2, 0, 6, 4, 3, 1, 7, 5), (2, 0, 6, 4, 3, 1, 7, 5), (4, 6, 0, 2, 5, 7, 1, 3), (4, 6, 0, 2, 5, 7, 1, 3), (6, 4, 2, 0, 7, 5, 3, 1), (6, 4, 2, 0, 7, 5, 3, 1))
TEXT_PLACE = ((6, 4, 2, 0, 7, 5, 3, 1), (0, 2, 4, 6, 1, 3, 5, 7), (0, 2, 4, 6, 1, 3, 5, 7), (2, 0, 6, 4, 3, 1, 7, 5), (2, 0, 6, 4, 3, 1, 7, 5), (4, 6, 0, 2, 5, 7, 1, 3), (4, 6, 0, 2, 5, 7, 1, 3), (6, 4, 2, 0, 7, 5, 3, 1))


def routes(place, shift):
    extent = tuple(SIZES[a] for a in MOVE_AXES)
    out = []
    for h, x, c, z in itertools.product(*map(range, extent)):
        pair = (8 * h + 2 * x + c + shift) % 16
        half, p = divmod(pair, 8)
        spot = place[p][z]
        to = (half, spot // 2, spot % 2, PLANE[p])
        out.append((int(np.ravel_multi_index((h, x, c, z), extent)), int(np.ravel_multi_index(to, extent))))
    return out


IMAGE_ROUTE = routes(IMAGE_PLACE, 0)
TEXT_ROUTE = routes(TEXT_PLACE, 1)


def back(route):
    return [(b, a) for a, b in route]


def pack(rows, ids):
    below = jnp.pad(ids.astype(jnp.bfloat16)[None, :], ((0, EXTRA - 1), (0, D - ROWS)))
    return jnp.concatenate([rows, below], axis=0)


def id_row(ref):
    total = None
    for k in range(4):
        part = ref[k, ROWS:, :].astype(jnp.float32)
        part = jnp.concatenate([part, jnp.zeros((EXTRA, GROUP - D), jnp.float32)], axis=1)
        part = part if k == 0 else pltpu.roll(part, k * ROWS, 1)
        total = part if total is None else total + part
    return total[0:1, :]


VMEM = pl.BlockSpec(memory_space=pltpu.VMEM)
SMEM = pl.BlockSpec(memory_space=pltpu.SMEM)


def call(kernel, name, out, in_specs, flops, *args):
    return pl.pallas_call(
        kernel,
        out_shape=tuple(jax.ShapeDtypeStruct(shape, kind) for shape, kind in out),
        in_specs=in_specs,
        out_specs=(VMEM,) * len(out),
        compiler_params=pltpu.CompilerParams(vmem_limit_bytes=24 * 1024 * 1024),
        cost_estimate=pl.CostEstimate(flops=flops, bytes_accessed=4 << 20, transcendentals=0),
        name=name,
    )(*args)


def pair_weights(scale_ref, block, texts, ids, text_ids):
    scores = lax.dot_general(block, texts, (((1,), (1,)), ((), ())), preferred_element_type=jnp.float32)
    scores = scores * scale_ref[0] + scale_ref[1]
    positive = (jnp.concatenate([ids] * (GROUP // 128), axis=1) == text_ids).astype(jnp.float32)
    return (jax.nn.sigmoid(scores) - positive).astype(jnp.bfloat16)


def unpack_rows(ref, rows):
    for k in range(4):
        rows[k * ROWS : (k + 1) * ROWS, :] = ref[k, :ROWS, :]


def id_tile(ids, j):
    return jnp.broadcast_to(ids[:, j * 128 : (j + 1) * 128], (128, 128)).T


def own_kernel(scale_ref, image_ref, text_ref, weights, images, texts, text_ids):
    unpack_rows(text_ref, texts)
    unpack_rows(image_ref, images)
    text_row = id_row(text_ref)
    text_ids[...] = jnp.broadcast_to(text_row, text_ids.shape)
    ids = id_row(image_ref)
    for j in range(GROUP // CHUNK):
        rows = pl.ds(j * CHUNK, CHUNK)
        columns = jnp.concatenate([id_tile(ids, 2 * j), id_tile(ids, 2 * j + 1)], axis=0)
        weights[rows, :] = pair_weights(scale_ref, images[rows, :], texts[...], columns, text_row)


def other_kernel(scale_ref, image_ref, texts, text_ids, weights, images):
    unpack_rows(image_ref, images)
    text_row = text_ids[0:1, :]
    ids = id_row(image_ref)
    for j in range(GROUP // CHUNK):
        rows = pl.ds(j * CHUNK, CHUNK)
        columns = jnp.concatenate([id_tile(ids, 2 * j), id_tile(ids, 2 * j + 1)], axis=0)
        weights[rows, :] = pair_weights(scale_ref, images[rows, :], texts[...], columns, text_row)


def other_grad_kernel(scale_ref, weights, texts, grads):
    for j in range(GROUP // CHUNK):
        rows = pl.ds(j * CHUNK, CHUNK)
        grad = jnp.dot(weights[rows, :], texts[...], preferred_element_type=jnp.float32)
        grads[rows, :] = (scale_ref[0] * 0.125 * grad).astype(grads.dtype)


def text_kernel(scale_ref, own_weights, own_images, other_weights, other_images, grads):
    fold = (((0,), (0,)), ((), ()))
    for j in range(GROUP // CHUNK):
        rows = pl.ds(j * CHUNK, CHUNK)
        grad = lax.dot_general(own_weights[:, rows], own_images[...], fold, preferred_element_type=jnp.float32)
        grad = grad + lax.dot_general(other_weights[:, rows], other_images[...], fold, preferred_element_type=jnp.float32)
        grads[rows, :] = (scale_ref[0] * 0.125 * grad).astype(grads.dtype)


def image_kernel(scale_ref, place_ref, weights, texts, received, kept, *sent):
    for k, out in enumerate((kept, *sent)):
        shard = lax.rem(place_ref[0] + k, 4)
        rows = pl.ds(pl.multiple_of(shard * ROWS, ROWS), ROWS)
        grad = jnp.dot(weights[rows, :], texts[...], preferred_element_type=jnp.float32)
        out[...] = (scale_ref[0] * 0.125 * grad + received[rows, :].astype(jnp.float32)).astype(out.dtype)


def body(picture_vectors, caption_vectors, picture_match_label, caption_match_label, inverse_softness, score_offset):
    scale = jnp.concatenate([inverse_softness, score_offset])
    place = lax.axis_index("x").astype(jnp.int32).reshape(1)
    packed_images = pack(picture_vectors, picture_match_label)
    packed_texts = pack(caption_vectors, caption_match_label)
    packed_images, packed_texts = lax.optimization_barrier((packed_images, packed_texts))
    images = lax.ppermute(packed_images, MOVE_AXES, IMAGE_ROUTE)
    texts = lax.ppermute(packed_texts, MOVE_AXES, TEXT_ROUTE)
    images, texts = lax.optimization_barrier((images, texts))
    own = lax.all_to_all(jnp.broadcast_to(images[None], (4, PACKED, D)), "x", split_axis=0, concat_axis=0, tiled=True)
    other = lax.ppermute(own, "c", [(0, 1), (1, 0)])
    text = lax.all_gather(texts, "y", axis=0)
    half, flops = (GROUP, GROUP), 2 * GROUP * GROUP * D
    rows = (GROUP, D)
    bf16, f32 = jnp.bfloat16, jnp.float32
    own_weights, own_images, all_texts, text_ids = call(
        own_kernel, "own_weights", ((half, bf16), (rows, bf16), (rows, bf16), ((8, GROUP), f32)), [SMEM, VMEM, VMEM], 40 * flops, scale, own, text
    )
    other_weights, other_images = call(
        other_kernel, "other_weights", ((half, bf16), (rows, bf16)), [SMEM, VMEM, VMEM, VMEM], flops, scale, other, all_texts, text_ids
    )
    (text_part,) = call(
        text_kernel, "text_grads", ((rows, bf16),), [SMEM] + [VMEM] * 4, 2 * flops, scale, own_weights, own_images, other_weights, other_images
    )
    text_parts = lax.all_to_all(text_part, "y", split_axis=0, concat_axis=0, tiled=True)
    (other_grad,) = call(other_grad_kernel, "other_grads", ((rows, bf16),), [SMEM, VMEM, VMEM], flops, scale, other_weights, all_texts)
    received = lax.ppermute(other_grad, "c", [(0, 1), (1, 0)])
    shard = (ROWS, D)
    kept, *sent = call(
        image_kernel, "image_grads", ((shard, f32),) + ((shard, bf16),) * 3, [SMEM, SMEM] + [VMEM] * 3, flops, scale, place, own_weights, all_texts, received
    )
    for k, part in enumerate(sent, 1):
        kept = kept + lax.ppermute(part, "x", [(i, (i + k) % 4) for i in range(4)]).astype(f32)
    image_home = lax.ppermute(kept.astype(bf16), MOVE_AXES, back(IMAGE_ROUTE))
    text_sum = jnp.sum(text_parts.reshape(4, ROWS, D).astype(f32), axis=0).astype(bf16)
    text_home = lax.ppermute(text_sum, MOVE_AXES, back(TEXT_ROUTE))
    return image_home, text_home.astype(f32)


def solution(mesh):
    fine = Mesh(mesh.devices.reshape(tuple(SIZES.values())), AXES)
    rows, ids = P(AXES, None), P(AXES)
    return jax.shard_map(
        body,
        mesh=fine,
        in_specs=(rows, rows, ids, ids, P(), P()),
        out_specs=(rows, rows),
        check_vma=False,
    )
```

```python
import itertools

import jax
import jax.numpy as jnp
import numpy as np
from jax import lax
from jax.experimental import pallas as pl
from jax.experimental.pallas import tpu as pltpu
from jax.sharding import Mesh, PartitionSpec as P

AXES = ("h", "x", "c", "y", "z")
SIZES = dict(h=2, x=4, c=2, y=4, z=8)
MOVE_AXES = ("h", "x", "c", "z")
ROWS = 192
EXTRA = 8
PACKED = ROWS + EXTRA
D = 640
GROUP = 4 * ROWS
CHUNK = 256

PLANE = (7, 3, 0, 5, 2, 6, 1, 4)
IMAGE_PLACE = ((0, 2, 4, 6, 1, 3, 5, 7), (0, 2, 4, 6, 1, 3, 5, 7), (2, 0, 6, 4, 3, 1, 7, 5), (2, 0, 6, 4, 3, 1, 7, 5), (4, 6, 0, 2, 5, 7, 1, 3), (4, 6, 0, 2, 5, 7, 1, 3), (6, 4, 2, 0, 7, 5, 3, 1), (6, 4, 2, 0, 7, 5, 3, 1))
TEXT_PLACE = ((6, 4, 2, 0, 7, 5, 3, 1), (0, 2, 4, 6, 1, 3, 5, 7), (0, 2, 4, 6, 1, 3, 5, 7), (2, 0, 6, 4, 3, 1, 7, 5), (2, 0, 6, 4, 3, 1, 7, 5), (4, 6, 0, 2, 5, 7, 1, 3), (4, 6, 0, 2, 5, 7, 1, 3), (6, 4, 2, 0, 7, 5, 3, 1))


def routes(place, shift):
    extent = tuple(SIZES[a] for a in MOVE_AXES)
    out = []
    for h, x, c, z in itertools.product(*map(range, extent)):
        pair = (8 * h + 2 * x + c + shift) % 16
        half, p = divmod(pair, 8)
        spot = place[p][z]
        to = (half, spot // 2, spot % 2, PLANE[p])
        out.append((int(np.ravel_multi_index((h, x, c, z), extent)), int(np.ravel_multi_index(to, extent))))
    return out


IMAGE_ROUTE = routes(IMAGE_PLACE, 0)
TEXT_ROUTE = routes(TEXT_PLACE, 1)


def back(route):
    return [(b, a) for a, b in route]


def pack(rows, ids):
    return jnp.concatenate([rows, jnp.pad(ids[None, :], ((0, EXTRA - 1), (0, D - ROWS)))], axis=0)


def id_row(ref):
    total = None
    for k in range(4):
        part = ref[k, ROWS:, :].astype(jnp.float32)
        part = jnp.concatenate([part, jnp.zeros((EXTRA, GROUP - D), jnp.float32)], axis=1)
        part = part if k == 0 else pltpu.roll(part, k * ROWS, 1)
        total = part if total is None else total + part
    return total[0:1, :]


VMEM = pl.BlockSpec(memory_space=pltpu.VMEM)
SMEM = pl.BlockSpec(memory_space=pltpu.SMEM)


def call(kernel, name, out, in_specs, flops, *args, scratch=()):
    return pl.pallas_call(
        kernel,
        out_shape=tuple(jax.ShapeDtypeStruct(shape, kind) for shape, kind in out),
        in_specs=in_specs,
        out_specs=(VMEM,) * len(out),
        scratch_shapes=list(scratch),
        compiler_params=pltpu.CompilerParams(vmem_limit_bytes=16 * 1024 * 1024),
        cost_estimate=pl.CostEstimate(flops=flops, bytes_accessed=4 << 20, transcendentals=0),
        name=name,
    )(*args)


def pair_weights(scale_ref, block, texts, ids, text_ids):
    scores = lax.dot_general(block, texts, (((1,), (1,)), ((), ())), preferred_element_type=jnp.float32)
    scores = scores * scale_ref[0] + scale_ref[1]
    positive = (jnp.concatenate([ids] * (GROUP // 128), axis=1) == text_ids).astype(jnp.float32)
    return (jax.nn.sigmoid(scores) - positive).astype(jnp.bfloat16)


def unpack_rows(ref, rows):
    for k in range(4):
        rows[k * ROWS : (k + 1) * ROWS, :] = ref[k, :ROWS, :]


def id_tile(ids, j):
    return jnp.broadcast_to(ids[:, j * 128 : (j + 1) * 128], (128, 128)).T


def own_kernel(scale_ref, image_ref, text_ref, weights, images, texts, text_ids):
    unpack_rows(text_ref, texts)
    unpack_rows(image_ref, images)
    text_row = id_row(text_ref)
    text_ids[...] = jnp.broadcast_to(text_row, text_ids.shape)
    ids = id_row(image_ref)
    for j in range(GROUP // CHUNK):
        rows = pl.ds(j * CHUNK, CHUNK)
        columns = jnp.concatenate([id_tile(ids, 2 * j), id_tile(ids, 2 * j + 1)], axis=0)
        weights[rows, :] = pair_weights(scale_ref, images[rows, :], texts[...], columns, text_row)


def other_kernel(scale_ref, image_ref, texts, text_ids, own_weights, own_images, image_grads, text_grads, images, weights):
    unpack_rows(image_ref, images)
    factor = scale_ref[0] * 0.125
    text_row = text_ids[0:1, :]
    ids = id_row(image_ref)
    for j in range(GROUP // CHUNK):
        rows = pl.ds(j * CHUNK, CHUNK)
        columns = jnp.concatenate([id_tile(ids, 2 * j), id_tile(ids, 2 * j + 1)], axis=0)
        weight = pair_weights(scale_ref, images[rows, :], texts[...], columns, text_row)
        weights[rows, :] = weight
        grad = jnp.dot(weight, texts[...], preferred_element_type=jnp.float32)
        image_grads[rows, :] = (factor * grad).astype(image_grads.dtype)
    fold = (((0,), (0,)), ((), ()))
    for j in range(GROUP // CHUNK):
        rows = pl.ds(j * CHUNK, CHUNK)
        grad = lax.dot_general(own_weights[:, rows], own_images[...], fold, preferred_element_type=jnp.float32)
        grad = grad + lax.dot_general(weights[:, rows], images[...], fold, preferred_element_type=jnp.float32)
        text_grads[rows, :] = (factor * grad).astype(text_grads.dtype)


def image_shard(scale_ref, shard, weights, texts, received):
    rows = pl.ds(pl.multiple_of(shard * ROWS, ROWS), ROWS)
    grad = jnp.dot(weights[rows, :], texts[...], preferred_element_type=jnp.float32)
    return scale_ref[0] * 0.125 * grad + received[rows, :].astype(jnp.float32)


def image_kernel(scale_ref, place_ref, weights, texts, received, *sent):
    for k, out in enumerate(sent, 1):
        out[...] = image_shard(scale_ref, lax.rem(place_ref[0] + k, 4), weights, texts, received).astype(out.dtype)


def image_sum_kernel(scale_ref, place_ref, weights, texts, received, *rest):
    *parts, out = rest
    total = image_shard(scale_ref, place_ref[0], weights, texts, received)
    for part in parts:
        total = total + part[...].astype(jnp.float32)
    out[...] = total.astype(out.dtype)


def body(picture_vectors, caption_vectors, picture_match_label, caption_match_label, inverse_softness, score_offset):
    scale = jnp.concatenate([inverse_softness, score_offset])
    place = lax.axis_index("x").astype(jnp.int32).reshape(1)
    labels = lax.optimization_barrier(jnp.stack([picture_match_label, caption_match_label]).astype(jnp.bfloat16))
    packed_images = pack(picture_vectors, labels[0])
    packed_texts = pack(caption_vectors, labels[1])
    packed_images, packed_texts = lax.optimization_barrier((packed_images, packed_texts))
    images = lax.ppermute(packed_images, MOVE_AXES, IMAGE_ROUTE)
    texts = lax.ppermute(packed_texts, MOVE_AXES, TEXT_ROUTE)
    images, texts = lax.optimization_barrier((images, texts))
    own = lax.all_to_all(jnp.broadcast_to(images[None], (4, PACKED, D)), "x", split_axis=0, concat_axis=0, tiled=True)
    other = lax.ppermute(own, "c", [(0, 1), (1, 0)])
    text = lax.all_gather(texts, "y", axis=0)
    half, flops = (GROUP, GROUP), 2 * GROUP * GROUP * D
    rows = (GROUP, D)
    bf16, f32 = jnp.bfloat16, jnp.float32
    own_weights, own_images, all_texts, text_ids = call(
        own_kernel, "own_weights", ((half, bf16), (rows, bf16), (rows, bf16), ((8, GROUP), f32)), [SMEM, VMEM, VMEM], 40 * flops, scale, own, text
    )
    other_grad, text_part = call(
        other_kernel, "other_grads", ((rows, bf16), (rows, bf16)), [SMEM] + [VMEM] * 5, 4 * flops, scale, other, all_texts, text_ids, own_weights, own_images,
        scratch=[pltpu.VMEM(rows, bf16), pltpu.VMEM(half, bf16)],
    )
    received = lax.ppermute(other_grad, "c", [(0, 1), (1, 0)])
    text_parts = lax.all_to_all(text_part, "y", split_axis=0, concat_axis=0, tiled=True)
    shard = ((ROWS, D), bf16)
    sent = call(image_kernel, "image_grads", (shard,) * 3, [SMEM, SMEM] + [VMEM] * 3, 0, scale, place, own_weights, all_texts, received)
    parts = [lax.ppermute(part, "x", [(i, (i + k) % 4) for i in range(4)]) for k, part in enumerate(sent, 1)]
    (kept,) = call(image_sum_kernel, "image_sum", (shard,), [SMEM, SMEM] + [VMEM] * 6, 0, scale, place, own_weights, all_texts, received, *parts)
    image_home = lax.ppermute(kept, MOVE_AXES, back(IMAGE_ROUTE))
    text_sum = sum(text_parts[k * ROWS : (k + 1) * ROWS].astype(f32) for k in range(4)).astype(bf16)
    text_home = lax.ppermute(text_sum, MOVE_AXES, back(TEXT_ROUTE))
    return image_home, text_home.astype(f32)


def solution(mesh):
    fine = Mesh(mesh.devices.reshape(tuple(SIZES.values())), AXES)
    rows, ids = P(AXES, None), P(AXES)
    return jax.shard_map(
        body,
        mesh=fine,
        in_specs=(rows, rows, ids, ids, P(), P()),
        out_specs=(rows, rows),
        check_vma=False,
    )
```

```python
import itertools

import jax
import jax.numpy as jnp
import numpy as np
from jax import lax
from jax.experimental import pallas as pl
from jax.experimental.pallas import tpu as pltpu
from jax.sharding import Mesh, PartitionSpec as P

AXES = ("h", "x", "c", "y", "z")
SIZES = dict(h=2, x=4, c=2, y=4, z=8)
MOVE_AXES = ("h", "x", "c", "z")
ROWS = 192
EXTRA = 8
PACKED = ROWS + EXTRA
D = 640
GROUP = 4 * ROWS
CHUNK = 256

PLANE = (7, 3, 0, 5, 2, 6, 1, 4)
IMAGE_PLACE = ((0, 2, 4, 6, 1, 3, 5, 7), (0, 2, 4, 6, 1, 3, 5, 7), (2, 0, 6, 4, 3, 1, 7, 5), (2, 0, 6, 4, 3, 1, 7, 5), (4, 6, 0, 2, 5, 7, 1, 3), (4, 6, 0, 2, 5, 7, 1, 3), (6, 4, 2, 0, 7, 5, 3, 1), (6, 4, 2, 0, 7, 5, 3, 1))
TEXT_PLACE = ((6, 4, 2, 0, 7, 5, 3, 1), (0, 2, 4, 6, 1, 3, 5, 7), (0, 2, 4, 6, 1, 3, 5, 7), (2, 0, 6, 4, 3, 1, 7, 5), (2, 0, 6, 4, 3, 1, 7, 5), (4, 6, 0, 2, 5, 7, 1, 3), (4, 6, 0, 2, 5, 7, 1, 3), (6, 4, 2, 0, 7, 5, 3, 1))


def routes(place, shift):
    extent = tuple(SIZES[a] for a in MOVE_AXES)
    out = []
    for h, x, c, z in itertools.product(*map(range, extent)):
        pair = (8 * h + 2 * x + c + shift) % 16
        half, p = divmod(pair, 8)
        spot = place[p][z]
        to = (half, spot // 2, spot % 2, PLANE[p])
        out.append((int(np.ravel_multi_index((h, x, c, z), extent)), int(np.ravel_multi_index(to, extent))))
    return out


IMAGE_ROUTE = routes(IMAGE_PLACE, 0)
TEXT_ROUTE = routes(TEXT_PLACE, 1)


def back(route):
    return [(b, a) for a, b in route]


def pack(rows, ids):
    below = jnp.broadcast_to(ids.astype(jnp.bfloat16)[None, :], (EXTRA, ROWS))
    return jnp.concatenate([rows, jnp.pad(below, ((0, 0), (0, D - ROWS)))], axis=0)


def id_row(ref):
    total = None
    for k in range(4):
        part = ref[k, ROWS:, :].astype(jnp.float32)
        part = jnp.concatenate([part, jnp.zeros((EXTRA, GROUP - D), jnp.float32)], axis=1)
        part = part if k == 0 else pltpu.roll(part, k * ROWS, 1)
        total = part if total is None else total + part
    return total[0:1, :]


VMEM = pl.BlockSpec(memory_space=pltpu.VMEM)
SMEM = pl.BlockSpec(memory_space=pltpu.SMEM)


def call(kernel, name, out, in_specs, flops, *args, scratch=()):
    return pl.pallas_call(
        kernel,
        out_shape=tuple(jax.ShapeDtypeStruct(shape, kind) for shape, kind in out),
        in_specs=in_specs,
        out_specs=(VMEM,) * len(out),
        scratch_shapes=list(scratch),
        compiler_params=pltpu.CompilerParams(vmem_limit_bytes=16 * 1024 * 1024),
        cost_estimate=pl.CostEstimate(flops=flops, bytes_accessed=4 << 20, transcendentals=0),
        name=name,
    )(*args)


def pair_weights(scale_ref, block, texts, ids, text_ids):
    scores = lax.dot_general(block, texts, (((1,), (1,)), ((), ())), preferred_element_type=jnp.float32)
    scores = scores * scale_ref[0] + scale_ref[1]
    positive = (jnp.concatenate([ids] * (GROUP // 128), axis=1) == text_ids).astype(jnp.float32)
    return (jax.nn.sigmoid(scores) - positive).astype(jnp.bfloat16)


def unpack_rows(ref, rows):
    for k in range(4):
        rows[k * ROWS : (k + 1) * ROWS, :] = ref[k, :ROWS, :]


def id_tile(ids, j):
    return jnp.broadcast_to(ids[:, j * 128 : (j + 1) * 128], (128, 128)).T


def unpack_kernel(text_ref, texts, text_ids):
    unpack_rows(text_ref, texts)
    text_ids[...] = jnp.broadcast_to(id_row(text_ref), text_ids.shape)


def own_kernel(scale_ref, image_ref, texts, text_ids, weights, images):
    unpack_rows(image_ref, images)
    text_row = text_ids[0:1, :]
    ids = id_row(image_ref)
    for j in range(GROUP // CHUNK):
        rows = pl.ds(j * CHUNK, CHUNK)
        columns = jnp.concatenate([id_tile(ids, 2 * j), id_tile(ids, 2 * j + 1)], axis=0)
        weights[rows, :] = pair_weights(scale_ref, images[rows, :], texts[...], columns, text_row)


def other_kernel(scale_ref, image_ref, texts, text_ids, own_weights, own_images, image_grads, text_grads, images, weights):
    unpack_rows(image_ref, images)
    factor = scale_ref[0] * 0.125
    text_row = text_ids[0:1, :]
    ids = id_row(image_ref)
    for j in range(GROUP // CHUNK):
        rows = pl.ds(j * CHUNK, CHUNK)
        columns = jnp.concatenate([id_tile(ids, 2 * j), id_tile(ids, 2 * j + 1)], axis=0)
        weight = pair_weights(scale_ref, images[rows, :], texts[...], columns, text_row)
        weights[rows, :] = weight
        grad = jnp.dot(weight, texts[...], preferred_element_type=jnp.float32)
        image_grads[rows, :] = (factor * grad).astype(image_grads.dtype)
    fold = (((0,), (0,)), ((), ()))
    for j in range(GROUP // CHUNK):
        rows = pl.ds(j * CHUNK, CHUNK)
        grad = lax.dot_general(own_weights[:, rows], own_images[...], fold, preferred_element_type=jnp.float32)
        grad = grad + lax.dot_general(weights[:, rows], images[...], fold, preferred_element_type=jnp.float32)
        text_grads[rows, :] = (factor * grad).astype(text_grads.dtype)


def image_shard(scale_ref, shard, weights, texts, received):
    rows = pl.ds(pl.multiple_of(shard * ROWS, ROWS), ROWS)
    grad = jnp.dot(weights[rows, :], texts[...], preferred_element_type=jnp.float32)
    return scale_ref[0] * 0.125 * grad + received[rows, :].astype(jnp.float32)


def image_kernel(scale_ref, place_ref, weights, texts, received, *sent):
    for k, out in enumerate(sent, 1):
        out[...] = image_shard(scale_ref, lax.rem(place_ref[0] + k, 4), weights, texts, received).astype(out.dtype)


def image_sum_kernel(scale_ref, place_ref, weights, texts, received, *rest):
    *parts, out = rest
    total = image_shard(scale_ref, place_ref[0], weights, texts, received)
    for part in parts:
        total = total + part[...].astype(jnp.float32)
    out[...] = total.astype(out.dtype)


def text_sum_kernel(parts, out):
    total = parts[0:ROWS, :].astype(jnp.float32)
    for k in range(1, 4):
        total = total + parts[k * ROWS : (k + 1) * ROWS, :].astype(jnp.float32)
    out[...] = total.astype(out.dtype)


def body(picture_vectors, caption_vectors, picture_match_label, caption_match_label, inverse_softness, score_offset):
    scale = jnp.concatenate([inverse_softness, score_offset])
    place = lax.axis_index("x").astype(jnp.int32).reshape(1)
    packed_images = pack(picture_vectors, picture_match_label)
    packed_texts = pack(caption_vectors, caption_match_label)
    packed_images, packed_texts = lax.optimization_barrier((packed_images, packed_texts))
    images = lax.ppermute(packed_images, MOVE_AXES, IMAGE_ROUTE)
    texts = lax.ppermute(packed_texts, MOVE_AXES, TEXT_ROUTE)
    own = lax.all_to_all(jnp.broadcast_to(images[None], (4, PACKED, D)), "x", split_axis=0, concat_axis=0, tiled=True)
    other = lax.ppermute(own, "c", [(0, 1), (1, 0)])
    text = lax.all_gather(texts, "y", axis=0)
    half, flops = (GROUP, GROUP), 2 * GROUP * GROUP * D
    rows = (GROUP, D)
    bf16, f32 = jnp.bfloat16, jnp.float32
    all_texts, text_ids = call(unpack_kernel, "unpack_texts", ((rows, bf16), ((8, GROUP), f32)), [VMEM], 40 * flops, text)
    own_weights, own_images = call(
        own_kernel, "own_weights", ((half, bf16), (rows, bf16)), [SMEM, VMEM, VMEM, VMEM], 40 * flops, scale, own, all_texts, text_ids
    )
    other_grad, text_part = call(
        other_kernel, "other_grads", ((rows, bf16), (rows, bf16)), [SMEM] + [VMEM] * 5, 4 * flops, scale, other, all_texts, text_ids, own_weights, own_images,
        scratch=[pltpu.VMEM(rows, bf16), pltpu.VMEM(half, bf16)],
    )
    received = lax.ppermute(other_grad, "c", [(0, 1), (1, 0)])
    text_parts = lax.all_to_all(text_part, "y", split_axis=0, concat_axis=0, tiled=True)
    shard = ((ROWS, D), bf16)
    sent = call(image_kernel, "image_grads", (shard,) * 3, [SMEM, SMEM] + [VMEM] * 3, 0, scale, place, own_weights, all_texts, received)
    parts = [lax.ppermute(part, "x", [(i, (i + k) % 4) for i in range(4)]) for k, part in enumerate(sent, 1)]
    (kept,) = call(image_sum_kernel, "image_sum", (shard,), [SMEM, SMEM] + [VMEM] * 6, 0, scale, place, own_weights, all_texts, received, *parts)
    image_home = lax.ppermute(kept, MOVE_AXES, back(IMAGE_ROUTE))
    (text_sum,) = call(text_sum_kernel, "text_sum", (shard,), [VMEM], 0, text_parts)
    text_home = lax.ppermute(text_sum, MOVE_AXES, back(TEXT_ROUTE))
    return image_home, text_home.astype(f32)


def solution(mesh):
    fine = Mesh(mesh.devices.reshape(tuple(SIZES.values())), AXES)
    rows, ids = P(AXES, None), P(AXES)
    return jax.shard_map(
        body,
        mesh=fine,
        in_specs=(rows, rows, ids, ids, P(), P()),
        out_specs=(rows, rows),
        check_vma=False,
    )
```

```python
import itertools

import jax
import jax.numpy as jnp
import numpy as np
from jax import lax
from jax.experimental import pallas as pl
from jax.experimental.pallas import tpu as pltpu
from jax.sharding import Mesh, PartitionSpec as P

AXES = ("h", "x", "c", "y", "z")
SIZES = dict(h=2, x=4, c=2, y=4, z=8)
MOVE_AXES = ("h", "x", "c", "z")
ROWS = 192
EXTRA = 8
PACKED = ROWS + EXTRA
D = 640
GROUP = 4 * ROWS
CHUNK = 256

PLANE = (7, 3, 0, 5, 2, 6, 1, 4)
IMAGE_PLACE = ((0, 2, 4, 6, 1, 3, 5, 7), (0, 2, 4, 6, 1, 3, 5, 7), (2, 0, 6, 4, 3, 1, 7, 5), (2, 0, 6, 4, 3, 1, 7, 5), (4, 6, 0, 2, 5, 7, 1, 3), (4, 6, 0, 2, 5, 7, 1, 3), (6, 4, 2, 0, 7, 5, 3, 1), (6, 4, 2, 0, 7, 5, 3, 1))
TEXT_PLACE = ((6, 4, 2, 0, 7, 5, 3, 1), (0, 2, 4, 6, 1, 3, 5, 7), (0, 2, 4, 6, 1, 3, 5, 7), (2, 0, 6, 4, 3, 1, 7, 5), (2, 0, 6, 4, 3, 1, 7, 5), (4, 6, 0, 2, 5, 7, 1, 3), (4, 6, 0, 2, 5, 7, 1, 3), (6, 4, 2, 0, 7, 5, 3, 1))


def routes(place, shift):
    extent = tuple(SIZES[a] for a in MOVE_AXES)
    out = []
    for h, x, c, z in itertools.product(*map(range, extent)):
        pair = (8 * h + 2 * x + c + shift) % 16
        half, p = divmod(pair, 8)
        spot = place[p][z]
        to = (half, spot // 2, spot % 2, PLANE[p])
        out.append((int(np.ravel_multi_index((h, x, c, z), extent)), int(np.ravel_multi_index(to, extent))))
    return out


IMAGE_ROUTE = routes(IMAGE_PLACE, 0)
TEXT_ROUTE = routes(TEXT_PLACE, 1)


def back(route):
    return [(b, a) for a, b in route]


def pack(rows, ids):
    below = jnp.broadcast_to(ids.astype(jnp.bfloat16)[None, :], (EXTRA, ROWS))
    return jnp.concatenate([rows, jnp.pad(below, ((0, 0), (0, D - ROWS)))], axis=0)


def id_row(ref):
    total = None
    for k in range(4):
        part = ref[k, ROWS:, :].astype(jnp.float32)
        part = jnp.concatenate([part, jnp.zeros((EXTRA, GROUP - D), jnp.float32)], axis=1)
        part = part if k == 0 else pltpu.roll(part, k * ROWS, 1)
        total = part if total is None else total + part
    return total[0:1, :]


VMEM = pl.BlockSpec(memory_space=pltpu.VMEM)
SMEM = pl.BlockSpec(memory_space=pltpu.SMEM)


def call(kernel, name, out, in_specs, flops, *args, scratch=()):
    return pl.pallas_call(
        kernel,
        out_shape=tuple(jax.ShapeDtypeStruct(shape, kind) for shape, kind in out),
        in_specs=in_specs,
        out_specs=(VMEM,) * len(out),
        scratch_shapes=list(scratch),
        compiler_params=pltpu.CompilerParams(vmem_limit_bytes=16 * 1024 * 1024),
        cost_estimate=pl.CostEstimate(flops=flops, bytes_accessed=4 << 20, transcendentals=0),
        name=name,
    )(*args)


def pair_weights(scale_ref, block, texts, ids, text_ids):
    scores = lax.dot_general(block, texts, (((1,), (1,)), ((), ())), preferred_element_type=jnp.float32)
    scores = scores * scale_ref[0] + scale_ref[1]
    positive = (jnp.concatenate([ids] * (GROUP // 128), axis=1) == text_ids).astype(jnp.float32)
    return (jax.nn.sigmoid(scores) - positive).astype(jnp.bfloat16)


def unpack_rows(ref, rows):
    for k in range(4):
        rows[k * ROWS : (k + 1) * ROWS, :] = ref[k, :ROWS, :]


def id_tile(ids, j):
    return jnp.broadcast_to(ids[:, j * 128 : (j + 1) * 128], (128, 128)).T


def unpack_kernel(text_ref, texts, text_ids):
    unpack_rows(text_ref, texts)
    text_ids[...] = jnp.broadcast_to(id_row(text_ref), text_ids.shape)


def own_kernel(scale_ref, image_ref, texts, text_ids, weights, images, text_sum):
    unpack_rows(image_ref, images)
    text_row = text_ids[0:1, :]
    ids = id_row(image_ref)
    for j in range(GROUP // CHUNK):
        rows = pl.ds(j * CHUNK, CHUNK)
        columns = jnp.concatenate([id_tile(ids, 2 * j), id_tile(ids, 2 * j + 1)], axis=0)
        weights[rows, :] = pair_weights(scale_ref, images[rows, :], texts[...], columns, text_row)
    fold = (((0,), (0,)), ((), ()))
    for j in range(GROUP // CHUNK):
        rows = pl.ds(j * CHUNK, CHUNK)
        text_sum[rows, :] = lax.dot_general(weights[:, rows], images[...], fold, preferred_element_type=jnp.float32)


def other_kernel(scale_ref, image_ref, texts, text_ids, text_sum, image_grads, text_grads, images, weights):
    unpack_rows(image_ref, images)
    factor = scale_ref[0] * 0.125
    text_row = text_ids[0:1, :]
    ids = id_row(image_ref)
    for j in range(GROUP // CHUNK):
        rows = pl.ds(j * CHUNK, CHUNK)
        columns = jnp.concatenate([id_tile(ids, 2 * j), id_tile(ids, 2 * j + 1)], axis=0)
        weight = pair_weights(scale_ref, images[rows, :], texts[...], columns, text_row)
        weights[rows, :] = weight
        grad = jnp.dot(weight, texts[...], preferred_element_type=jnp.float32)
        image_grads[rows, :] = (factor * grad).astype(image_grads.dtype)
    fold = (((0,), (0,)), ((), ()))
    for j in range(GROUP // CHUNK):
        rows = pl.ds(j * CHUNK, CHUNK)
        grad = text_sum[rows, :] + lax.dot_general(weights[:, rows], images[...], fold, preferred_element_type=jnp.float32)
        text_grads[rows, :] = (factor * grad).astype(text_grads.dtype)


def image_shard(scale_ref, shard, weights, texts, received):
    rows = pl.ds(pl.multiple_of(shard * ROWS, ROWS), ROWS)
    grad = jnp.dot(weights[rows, :], texts[...], preferred_element_type=jnp.float32)
    return scale_ref[0] * 0.125 * grad + received[rows, :].astype(jnp.float32)


def image_kernel(scale_ref, place_ref, weights, texts, received, *sent):
    for k, out in enumerate(sent, 1):
        out[...] = image_shard(scale_ref, lax.rem(place_ref[0] + k, 4), weights, texts, received).astype(out.dtype)


def image_sum_kernel(scale_ref, place_ref, weights, texts, received, *rest):
    *parts, out = rest
    total = image_shard(scale_ref, place_ref[0], weights, texts, received)
    for part in parts:
        total = total + part[...].astype(jnp.float32)
    out[...] = total.astype(out.dtype)


def text_sum_kernel(parts, out):
    total = parts[0:ROWS, :].astype(jnp.float32)
    for k in range(1, 4):
        total = total + parts[k * ROWS : (k + 1) * ROWS, :].astype(jnp.float32)
    out[...] = total.astype(out.dtype)


def body(picture_vectors, caption_vectors, picture_match_label, caption_match_label, inverse_softness, score_offset):
    scale = jnp.concatenate([inverse_softness, score_offset])
    place = lax.axis_index("x").astype(jnp.int32).reshape(1)
    packed_images = pack(picture_vectors, picture_match_label)
    packed_texts = pack(caption_vectors, caption_match_label)
    images = lax.ppermute(packed_images, MOVE_AXES, IMAGE_ROUTE)
    texts = lax.ppermute(packed_texts, MOVE_AXES, TEXT_ROUTE)
    own = lax.all_to_all(jnp.broadcast_to(images[None], (4, PACKED, D)), "x", split_axis=0, concat_axis=0, tiled=True)
    other = lax.ppermute(own, "c", [(0, 1), (1, 0)])
    text = lax.all_gather(texts, "y", axis=0)
    half, flops = (GROUP, GROUP), 2 * GROUP * GROUP * D
    rows = (GROUP, D)
    bf16, f32 = jnp.bfloat16, jnp.float32
    all_texts, text_ids = call(unpack_kernel, "unpack_texts", ((rows, bf16), ((8, GROUP), f32)), [VMEM], 40 * flops, text)
    own_weights, _, own_text = call(
        own_kernel, "own_weights", ((half, bf16), (rows, bf16), (rows, f32)), [SMEM, VMEM, VMEM, VMEM], 40 * flops, scale, own, all_texts, text_ids
    )
    other_grad, text_part = call(
        other_kernel, "other_grads", ((rows, bf16), (rows, bf16)), [SMEM] + [VMEM] * 4, 4 * flops, scale, other, all_texts, text_ids, own_text,
        scratch=[pltpu.VMEM(rows, bf16), pltpu.VMEM(half, bf16)],
    )
    received = lax.ppermute(other_grad, "c", [(0, 1), (1, 0)])
    text_parts = lax.all_to_all(text_part, "y", split_axis=0, concat_axis=0, tiled=True)
    shard = ((ROWS, D), bf16)
    sent = call(image_kernel, "image_grads", (shard,) * 3, [SMEM, SMEM] + [VMEM] * 3, 0, scale, place, own_weights, all_texts, received)
    parts = [lax.ppermute(part, "x", [(i, (i + k) % 4) for i in range(4)]) for k, part in enumerate(sent, 1)]
    (kept,) = call(image_sum_kernel, "image_sum", (shard,), [SMEM, SMEM] + [VMEM] * 6, 0, scale, place, own_weights, all_texts, received, *parts)
    image_home = lax.ppermute(kept, MOVE_AXES, back(IMAGE_ROUTE))
    (text_sum,) = call(text_sum_kernel, "text_sum", (shard,), [VMEM], 0, text_parts)
    text_home = lax.ppermute(text_sum, MOVE_AXES, back(TEXT_ROUTE))
    return image_home, text_home.astype(f32)


def solution(mesh):
    fine = Mesh(mesh.devices.reshape(tuple(SIZES.values())), AXES)
    rows, ids = P(AXES, None), P(AXES)
    return jax.shard_map(
        body,
        mesh=fine,
        in_specs=(rows, rows, ids, ids, P(), P()),
        out_specs=(rows, rows),
        check_vma=False,
    )
```

```python
import itertools

import jax
import jax.numpy as jnp
import numpy as np
from jax import lax
from jax.experimental import pallas as pl
from jax.experimental.pallas import tpu as pltpu
from jax.sharding import Mesh, PartitionSpec as P

AXES = ("h", "x", "c", "y", "z")
SIZES = dict(h=2, x=4, c=2, y=4, z=8)
MOVE_AXES = ("h", "x", "c", "z")
ROWS = 192
EXTRA = 8
PACKED = ROWS + EXTRA
D = 640
GROUP = 4 * ROWS
CHUNK = 256

PLANE = (7, 3, 0, 5, 2, 6, 1, 4)
IMAGE_PLACE = ((0, 2, 4, 6, 1, 3, 5, 7), (0, 2, 4, 6, 1, 3, 5, 7), (2, 0, 6, 4, 3, 1, 7, 5), (2, 0, 6, 4, 3, 1, 7, 5), (4, 6, 0, 2, 5, 7, 1, 3), (4, 6, 0, 2, 5, 7, 1, 3), (6, 4, 2, 0, 7, 5, 3, 1), (6, 4, 2, 0, 7, 5, 3, 1))
TEXT_PLACE = ((6, 4, 2, 0, 7, 5, 3, 1), (0, 2, 4, 6, 1, 3, 5, 7), (0, 2, 4, 6, 1, 3, 5, 7), (2, 0, 6, 4, 3, 1, 7, 5), (2, 0, 6, 4, 3, 1, 7, 5), (4, 6, 0, 2, 5, 7, 1, 3), (4, 6, 0, 2, 5, 7, 1, 3), (6, 4, 2, 0, 7, 5, 3, 1))


def routes(place, shift):
    extent = tuple(SIZES[a] for a in MOVE_AXES)
    out = []
    for h, x, c, z in itertools.product(*map(range, extent)):
        pair = (8 * h + 2 * x + c + shift) % 16
        half, p = divmod(pair, 8)
        spot = place[p][z]
        to = (half, spot // 2, spot % 2, PLANE[p])
        out.append((int(np.ravel_multi_index((h, x, c, z), extent)), int(np.ravel_multi_index(to, extent))))
    return out


IMAGE_ROUTE = routes(IMAGE_PLACE, 0)
TEXT_ROUTE = routes(TEXT_PLACE, 1)


def back(route):
    return [(b, a) for a, b in route]


def pack(rows, ids):
    below = jnp.broadcast_to(ids.astype(jnp.bfloat16)[None, :], (EXTRA, ROWS))
    return jnp.concatenate([rows, jnp.pad(below, ((0, 0), (0, D - ROWS)))], axis=0)


def id_row(ref):
    total = None
    for k in range(4):
        part = ref[k][ROWS:, :].astype(jnp.float32)
        part = jnp.concatenate([part, jnp.zeros((EXTRA, GROUP - D), jnp.float32)], axis=1)
        part = part if k == 0 else pltpu.roll(part, k * ROWS, 1)
        total = part if total is None else total + part
    return total[0:1, :]


VMEM = pl.BlockSpec(memory_space=pltpu.VMEM)
SMEM = pl.BlockSpec(memory_space=pltpu.SMEM)


def call(kernel, name, out, in_specs, flops, *args, scratch=()):
    return pl.pallas_call(
        kernel,
        out_shape=tuple(jax.ShapeDtypeStruct(shape, kind) for shape, kind in out),
        in_specs=in_specs,
        out_specs=(VMEM,) * len(out),
        scratch_shapes=list(scratch),
        compiler_params=pltpu.CompilerParams(vmem_limit_bytes=16 * 1024 * 1024),
        cost_estimate=pl.CostEstimate(flops=flops, bytes_accessed=4 << 20, transcendentals=0),
        name=name,
    )(*args)


def pair_weights(scale_ref, block, texts, ids, text_ids):
    scores = lax.dot_general(block, texts, (((1,), (1,)), ((), ())), preferred_element_type=jnp.float32)
    scores = scores * scale_ref[0] + scale_ref[1]
    positive = (jnp.concatenate([ids] * (GROUP // 128), axis=1) == text_ids).astype(jnp.float32)
    return (jax.nn.sigmoid(scores) - positive).astype(jnp.bfloat16)


def unpack_rows(ref, rows):
    for k in range(4):
        rows[k * ROWS : (k + 1) * ROWS, :] = ref[k, :ROWS, :]


def id_tile(ids, j):
    return jnp.broadcast_to(ids[:, j * 128 : (j + 1) * 128], (128, 128)).T


def unpack_kernel(text_ref, texts, text_ids):
    unpack_rows(text_ref, texts)
    text_ids[...] = jnp.broadcast_to(id_row(text_ref), text_ids.shape)


def own_kernel(scale_ref, image_ref, texts, text_ids, weights, images, text_sum):
    unpack_rows(image_ref, images)
    text_row = text_ids[0:1, :]
    ids = id_row(image_ref)
    for j in range(GROUP // CHUNK):
        rows = pl.ds(j * CHUNK, CHUNK)
        columns = jnp.concatenate([id_tile(ids, 2 * j), id_tile(ids, 2 * j + 1)], axis=0)
        weights[rows, :] = pair_weights(scale_ref, images[rows, :], texts[...], columns, text_row)
    fold = (((0,), (0,)), ((), ()))
    for j in range(GROUP // CHUNK):
        rows = pl.ds(j * CHUNK, CHUNK)
        text_sum[rows, :] = lax.dot_general(weights[:, rows], images[...], fold, preferred_element_type=jnp.float32)


def other_kernel(scale_ref, image_ref, texts, text_ids, text_sum, image_grads, text_grads, images, weights):
    unpack_rows(image_ref, images)
    factor = scale_ref[0] * 0.125
    text_row = text_ids[0:1, :]
    ids = id_row(image_ref)
    for j in range(GROUP // CHUNK):
        rows = pl.ds(j * CHUNK, CHUNK)
        columns = jnp.concatenate([id_tile(ids, 2 * j), id_tile(ids, 2 * j + 1)], axis=0)
        weight = pair_weights(scale_ref, images[rows, :], texts[...], columns, text_row)
        weights[rows, :] = weight
        grad = jnp.dot(weight, texts[...], preferred_element_type=jnp.float32)
        image_grads[rows, :] = (factor * grad).astype(image_grads.dtype)
    fold = (((0,), (0,)), ((), ()))
    for j in range(GROUP // CHUNK):
        rows = pl.ds(j * CHUNK, CHUNK)
        grad = text_sum[rows, :] + lax.dot_general(weights[:, rows], images[...], fold, preferred_element_type=jnp.float32)
        text_grads[rows, :] = (factor * grad).astype(text_grads.dtype)


def image_shard(scale_ref, shard, weights, texts, received):
    rows = pl.ds(pl.multiple_of(shard * ROWS, ROWS), ROWS)
    grad = jnp.dot(weights[rows, :], texts[...], preferred_element_type=jnp.float32)
    return scale_ref[0] * 0.125 * grad + received[rows, :].astype(jnp.float32)


def image_kernel(scale_ref, place_ref, weights, texts, received, *sent):
    for k, out in enumerate(sent, 1):
        out[...] = image_shard(scale_ref, lax.rem(place_ref[0] + k, 4), weights, texts, received).astype(out.dtype)


def image_sum_kernel(scale_ref, place_ref, weights, texts, received, *rest):
    *parts, out = rest
    total = image_shard(scale_ref, place_ref[0], weights, texts, received)
    for part in parts:
        total = total + part[...].astype(jnp.float32)
    out[...] = total.astype(out.dtype)


def text_sum_kernel(parts, out):
    total = parts[0:ROWS, :].astype(jnp.float32)
    for k in range(1, 4):
        total = total + parts[k * ROWS : (k + 1) * ROWS, :].astype(jnp.float32)
    out[...] = total.astype(out.dtype)


def body(picture_vectors, caption_vectors, picture_match_label, caption_match_label, inverse_softness, score_offset):
    scale = jnp.concatenate([inverse_softness, score_offset])
    place = lax.axis_index("x").astype(jnp.int32).reshape(1)
    packed_images = pack(picture_vectors, picture_match_label)
    packed_texts = pack(caption_vectors, caption_match_label)
    images = lax.ppermute(packed_images, MOVE_AXES, IMAGE_ROUTE)
    texts = lax.ppermute(packed_texts, MOVE_AXES, TEXT_ROUTE)
    own = lax.all_to_all(jnp.broadcast_to(images[None], (4, PACKED, D)), "x", split_axis=0, concat_axis=0, tiled=True)
    other = lax.ppermute(own, "c", [(0, 1), (1, 0)])
    text = lax.all_gather(texts, "y", axis=0)
    half, flops = (GROUP, GROUP), 2 * GROUP * GROUP * D
    rows = (GROUP, D)
    bf16, f32 = jnp.bfloat16, jnp.float32
    all_texts, text_ids = call(unpack_kernel, "unpack_texts", ((rows, bf16), ((8, GROUP), f32)), [VMEM], 40 * flops, text)
    own_weights, _, own_text = call(
        own_kernel, "own_weights", ((half, bf16), (rows, bf16), (rows, f32)), [SMEM, VMEM, VMEM, VMEM], 40 * flops, scale, own, all_texts, text_ids
    )
    other_grad, text_part = call(
        other_kernel, "other_grads", ((rows, bf16), (rows, bf16)), [SMEM] + [VMEM] * 4, 4 * flops, scale, other, all_texts, text_ids, own_text,
        scratch=[pltpu.VMEM(rows, bf16), pltpu.VMEM(half, bf16)],
    )
    received = lax.ppermute(other_grad, "c", [(0, 1), (1, 0)])
    text_parts = lax.all_to_all(text_part, "y", split_axis=0, concat_axis=0, tiled=True)
    shard = ((ROWS, D), bf16)
    sent = call(image_kernel, "image_grads", (shard,) * 3, [SMEM, SMEM] + [VMEM] * 3, 0, scale, place, own_weights, all_texts, received)
    parts = [lax.ppermute(part, "x", [(i, (i + k) % 4) for i in range(4)]) for k, part in enumerate(sent, 1)]
    (kept,) = call(image_sum_kernel, "image_sum", (shard,), [SMEM, SMEM] + [VMEM] * 6, 0, scale, place, own_weights, all_texts, received, *parts)
    image_home = lax.ppermute(kept, MOVE_AXES, back(IMAGE_ROUTE))
    (text_sum,) = call(text_sum_kernel, "text_sum", (shard,), [VMEM], 0, text_parts)
    text_home = lax.ppermute(text_sum, MOVE_AXES, back(TEXT_ROUTE))
    return image_home, text_home.astype(f32)


def solution(mesh):
    fine = Mesh(mesh.devices.reshape(tuple(SIZES.values())), AXES)
    rows, ids = P(AXES, None), P(AXES)
    return jax.shard_map(
        body,
        mesh=fine,
        in_specs=(rows, rows, ids, ids, P(), P()),
        out_specs=(rows, rows),
        check_vma=False,
    )
```

```python
import itertools

import jax
import jax.numpy as jnp
import numpy as np
from jax import lax
from jax.experimental import pallas as pl
from jax.experimental.pallas import tpu as pltpu
from jax.sharding import Mesh, PartitionSpec as P

AXES = ("h", "x", "c", "y", "z")
SIZES = dict(h=2, x=4, c=2, y=4, z=8)
MOVE_AXES = ("h", "x", "c", "z")
ROWS = 192
EXTRA = 8
PACKED = ROWS + EXTRA
D = 640
GROUP = 4 * ROWS
CHUNK = 256

PLANE = (7, 3, 0, 5, 2, 6, 1, 4)
IMAGE_PLACE = ((0, 2, 4, 6, 1, 3, 5, 7), (0, 2, 4, 6, 1, 3, 5, 7), (2, 0, 6, 4, 3, 1, 7, 5), (2, 0, 6, 4, 3, 1, 7, 5), (4, 6, 0, 2, 5, 7, 1, 3), (4, 6, 0, 2, 5, 7, 1, 3), (6, 4, 2, 0, 7, 5, 3, 1), (6, 4, 2, 0, 7, 5, 3, 1))
TEXT_PLACE = ((6, 4, 2, 0, 7, 5, 3, 1), (0, 2, 4, 6, 1, 3, 5, 7), (0, 2, 4, 6, 1, 3, 5, 7), (2, 0, 6, 4, 3, 1, 7, 5), (2, 0, 6, 4, 3, 1, 7, 5), (4, 6, 0, 2, 5, 7, 1, 3), (4, 6, 0, 2, 5, 7, 1, 3), (6, 4, 2, 0, 7, 5, 3, 1))


def routes(place, shift):
    extent = tuple(SIZES[a] for a in MOVE_AXES)
    out = []
    for h, x, c, z in itertools.product(*map(range, extent)):
        pair = (8 * h + 2 * x + c + shift) % 16
        half, p = divmod(pair, 8)
        spot = place[p][z]
        to = (half, spot // 2, spot % 2, PLANE[p])
        out.append((int(np.ravel_multi_index((h, x, c, z), extent)), int(np.ravel_multi_index(to, extent))))
    return out


IMAGE_ROUTE = routes(IMAGE_PLACE, 0)
TEXT_ROUTE = routes(TEXT_PLACE, 1)


def back(route):
    return [(b, a) for a, b in route]


def pack(rows, ids):
    below = jnp.broadcast_to(ids.astype(jnp.bfloat16)[None, :], (EXTRA, ROWS))
    return jnp.concatenate([rows, jnp.pad(below, ((0, 0), (0, D - ROWS)))], axis=0)


def id_row(ref):
    total = None
    for k in range(4):
        part = ref[k][ROWS:, :].astype(jnp.float32)
        part = jnp.concatenate([part, jnp.zeros((EXTRA, GROUP - D), jnp.float32)], axis=1)
        part = part if k == 0 else pltpu.roll(part, k * ROWS, 1)
        total = part if total is None else total + part
    return total[0:1, :]


VMEM = pl.BlockSpec(memory_space=pltpu.VMEM)
SMEM = pl.BlockSpec(memory_space=pltpu.SMEM)


def call(kernel, name, out, in_specs, flops, *args, scratch=()):
    return pl.pallas_call(
        kernel,
        out_shape=tuple(jax.ShapeDtypeStruct(shape, kind) for shape, kind in out),
        in_specs=in_specs,
        out_specs=(VMEM,) * len(out),
        scratch_shapes=list(scratch),
        compiler_params=pltpu.CompilerParams(vmem_limit_bytes=16 * 1024 * 1024),
        cost_estimate=pl.CostEstimate(flops=flops, bytes_accessed=4 << 20, transcendentals=0),
        name=name,
    )(*args)


def pair_weights(scale_ref, block, texts, ids, text_ids):
    scores = lax.dot_general(block, texts, (((1,), (1,)), ((), ())), preferred_element_type=jnp.float32)
    scores = scores * scale_ref[0] + scale_ref[1]
    positive = (jnp.concatenate([ids] * (GROUP // 128), axis=1) == text_ids).astype(jnp.float32)
    return (jax.nn.sigmoid(scores) - positive).astype(jnp.bfloat16)


def unpack_rows(ref, rows):
    for k in range(4):
        rows[k * ROWS : (k + 1) * ROWS, :] = ref[k, :ROWS, :]


def id_tile(ids, j):
    return jnp.broadcast_to(ids[:, j * 128 : (j + 1) * 128], (128, 128)).T


def unpack_kernel(text_ref, texts, text_ids):
    unpack_rows(text_ref, texts)
    text_ids[...] = jnp.broadcast_to(id_row(text_ref), text_ids.shape)


def own_kernel(scale_ref, image_ref, texts, text_ids, weights, images, text_sum):
    unpack_rows(image_ref, images)
    text_row = text_ids[0:1, :]
    ids = id_row(image_ref)
    for j in range(GROUP // CHUNK):
        rows = pl.ds(j * CHUNK, CHUNK)
        columns = jnp.concatenate([id_tile(ids, 2 * j), id_tile(ids, 2 * j + 1)], axis=0)
        weights[rows, :] = pair_weights(scale_ref, images[rows, :], texts[...], columns, text_row)
    fold = (((0,), (0,)), ((), ()))
    for j in range(GROUP // CHUNK):
        rows = pl.ds(j * CHUNK, CHUNK)
        text_sum[rows, :] = lax.dot_general(weights[:, rows], images[...], fold, preferred_element_type=jnp.float32)


def other_kernel(scale_ref, image_ref, texts, text_ids, text_sum, image_grads, text_grads, images, weights):
    unpack_rows(image_ref, images)
    factor = scale_ref[0] * 0.125
    text_row = text_ids[0:1, :]
    ids = id_row(image_ref)
    for j in range(GROUP // CHUNK):
        rows = pl.ds(j * CHUNK, CHUNK)
        columns = jnp.concatenate([id_tile(ids, 2 * j), id_tile(ids, 2 * j + 1)], axis=0)
        weight = pair_weights(scale_ref, images[rows, :], texts[...], columns, text_row)
        weights[rows, :] = weight
        grad = jnp.dot(weight, texts[...], preferred_element_type=jnp.float32)
        image_grads[rows, :] = (factor * grad).astype(image_grads.dtype)
    fold = (((0,), (0,)), ((), ()))
    for j in range(GROUP // CHUNK):
        rows = pl.ds(j * CHUNK, CHUNK)
        grad = text_sum[rows, :] + lax.dot_general(weights[:, rows], images[...], fold, preferred_element_type=jnp.float32)
        text_grads[rows, :] = (factor * grad).astype(text_grads.dtype)


def image_shard(scale_ref, shard, weights, texts, received):
    rows = pl.ds(pl.multiple_of(shard * ROWS, ROWS), ROWS)
    grad = jnp.dot(weights[rows, :], texts[...], preferred_element_type=jnp.float32)
    return scale_ref[0] * 0.125 * grad + received[rows, :].astype(jnp.float32)


def image_kernel(scale_ref, place_ref, weights, texts, received, *sent):
    for k, out in enumerate(sent, 1):
        out[...] = image_shard(scale_ref, lax.rem(place_ref[0] + k, 4), weights, texts, received).astype(out.dtype)


def image_sum_kernel(scale_ref, place_ref, weights, texts, received, *rest):
    *parts, out = rest
    total = image_shard(scale_ref, place_ref[0], weights, texts, received)
    for part in parts:
        total = total + part[...].astype(jnp.float32)
    out[...] = total.astype(out.dtype)


def text_sum_kernel(parts, out):
    total = parts[0:ROWS, :].astype(jnp.float32)
    for k in range(1, 4):
        total = total + parts[k * ROWS : (k + 1) * ROWS, :].astype(jnp.float32)
    out[...] = total.astype(out.dtype)


def body(picture_vectors, caption_vectors, picture_match_label, caption_match_label, inverse_softness, score_offset):
    scale = jnp.concatenate([inverse_softness, score_offset])
    place = lax.axis_index("x").astype(jnp.int32).reshape(1)
    packed_images = pack(picture_vectors, picture_match_label)
    packed_texts = pack(caption_vectors, caption_match_label)
    images = lax.ppermute(packed_images, MOVE_AXES, IMAGE_ROUTE)
    texts = lax.ppermute(packed_texts, MOVE_AXES, TEXT_ROUTE)
    own = lax.all_to_all(jnp.broadcast_to(images[None], (4, PACKED, D)), "x", split_axis=0, concat_axis=0, tiled=True)
    other = lax.ppermute(own, "c", [(0, 1), (1, 0)])
    text = lax.all_gather(texts, "y", axis=0)
    half, flops = (GROUP, GROUP), 2 * GROUP * GROUP * D
    rows = (GROUP, D)
    bf16, f32 = jnp.bfloat16, jnp.float32
    all_texts, text_ids = call(unpack_kernel, "unpack_texts", ((rows, bf16), ((8, GROUP), f32)), [VMEM], 40 * flops, text)
    own_weights, _, own_text = call(
        own_kernel, "own_weights", ((half, bf16), (rows, bf16), (rows, f32)), [SMEM, VMEM, VMEM, VMEM], 40 * flops, scale, own, all_texts, text_ids
    )
    other_grad, text_part = call(
        other_kernel, "other_grads", ((rows, bf16), (rows, bf16)), [SMEM] + [VMEM] * 4, 4 * flops, scale, other, all_texts, text_ids, own_text,
        scratch=[pltpu.VMEM(rows, bf16), pltpu.VMEM(half, bf16)],
    )
    received = lax.ppermute(other_grad, "c", [(0, 1), (1, 0)])
    text_parts = lax.all_to_all(text_part, "y", split_axis=0, concat_axis=0, tiled=True)
    shard = ((ROWS, D), bf16)
    sent = call(image_kernel, "image_grads", (shard,) * 3, [SMEM, SMEM] + [VMEM] * 3, 40 * flops, scale, place, own_weights, all_texts, received)
    parts = [lax.ppermute(part, "x", [(i, (i + k) % 4) for i in range(4)]) for k, part in enumerate(sent, 1)]
    (kept,) = call(image_sum_kernel, "image_sum", (shard,), [SMEM, SMEM] + [VMEM] * 6, 0, scale, place, own_weights, all_texts, received, *parts)
    image_home = lax.ppermute(kept, MOVE_AXES, back(IMAGE_ROUTE))
    (text_sum,) = call(text_sum_kernel, "text_sum", (shard,), [VMEM], 0, text_parts)
    text_home = lax.ppermute(text_sum, MOVE_AXES, back(TEXT_ROUTE))
    return image_home, text_home.astype(f32)


def solution(mesh):
    fine = Mesh(mesh.devices.reshape(tuple(SIZES.values())), AXES)
    rows, ids = P(AXES, None), P(AXES)
    return jax.shard_map(
        body,
        mesh=fine,
        in_specs=(rows, rows, ids, ids, P(), P()),
        out_specs=(rows, rows),
        check_vma=False,
    )
```

```python
import itertools

import jax
import jax.numpy as jnp
import numpy as np
from jax import lax
from jax.experimental import pallas as pl
from jax.experimental.pallas import tpu as pltpu
from jax.sharding import Mesh, PartitionSpec as P

AXES = ("h", "x", "c", "y", "z")
SIZES = dict(h=2, x=4, c=2, y=4, z=8)
MOVE_AXES = ("h", "x", "c", "z")
ROWS = 192
EXTRA = 8
PACKED = ROWS + EXTRA
D = 640
GROUP = 4 * ROWS
CHUNK = 256
STEPS = (2, 1, 3)

PLANE = (7, 3, 0, 5, 2, 6, 1, 4)
IMAGE_PLACE = ((0, 2, 4, 6, 1, 3, 5, 7), (0, 2, 4, 6, 1, 3, 5, 7), (2, 0, 6, 4, 3, 1, 7, 5), (2, 0, 6, 4, 3, 1, 7, 5), (4, 6, 0, 2, 5, 7, 1, 3), (4, 6, 0, 2, 5, 7, 1, 3), (6, 4, 2, 0, 7, 5, 3, 1), (6, 4, 2, 0, 7, 5, 3, 1))
TEXT_PLACE = ((6, 4, 2, 0, 7, 5, 3, 1), (0, 2, 4, 6, 1, 3, 5, 7), (0, 2, 4, 6, 1, 3, 5, 7), (2, 0, 6, 4, 3, 1, 7, 5), (2, 0, 6, 4, 3, 1, 7, 5), (4, 6, 0, 2, 5, 7, 1, 3), (4, 6, 0, 2, 5, 7, 1, 3), (6, 4, 2, 0, 7, 5, 3, 1))


def routes(place, shift):
    extent = tuple(SIZES[a] for a in MOVE_AXES)
    out = []
    for h, x, c, z in itertools.product(*map(range, extent)):
        pair = (8 * h + 2 * x + c + shift) % 16
        half, p = divmod(pair, 8)
        spot = place[p][z]
        to = (half, spot // 2, spot % 2, PLANE[p])
        out.append((int(np.ravel_multi_index((h, x, c, z), extent)), int(np.ravel_multi_index(to, extent))))
    return out


IMAGE_ROUTE = routes(IMAGE_PLACE, 0)
TEXT_ROUTE = routes(TEXT_PLACE, 1)


def back(route):
    return [(b, a) for a, b in route]


def pack(rows, ids):
    row = lax.optimization_barrier(ids[None, :])
    below = jnp.broadcast_to(row.astype(jnp.bfloat16), (EXTRA, ROWS))
    return jnp.concatenate([rows, jnp.pad(below, ((0, 0), (0, D - ROWS)))], axis=0)


def id_row(ref):
    total = None
    for k in range(4):
        part = ref[k][ROWS:, :].astype(jnp.float32)
        part = jnp.concatenate([part, jnp.zeros((EXTRA, GROUP - D), jnp.float32)], axis=1)
        part = part if k == 0 else pltpu.roll(part, k * ROWS, 1)
        total = part if total is None else total + part
    return total[0:1, :]


VMEM = pl.BlockSpec(memory_space=pltpu.VMEM)
SMEM = pl.BlockSpec(memory_space=pltpu.SMEM)


def call(kernel, name, out, in_specs, flops, *args, scratch=()):
    return pl.pallas_call(
        kernel,
        out_shape=tuple(jax.ShapeDtypeStruct(shape, kind) for shape, kind in out),
        in_specs=in_specs,
        out_specs=(VMEM,) * len(out),
        scratch_shapes=list(scratch),
        compiler_params=pltpu.CompilerParams(vmem_limit_bytes=16 * 1024 * 1024),
        cost_estimate=pl.CostEstimate(flops=flops, bytes_accessed=4 << 20, transcendentals=0),
        name=name,
    )(*args)


def pair_weights(scale_ref, block, texts, ids, text_ids):
    scores = lax.dot_general(block, texts, (((1,), (1,)), ((), ())), preferred_element_type=jnp.float32)
    scores = scores * scale_ref[0] + scale_ref[1]
    positive = (jnp.concatenate([ids] * (GROUP // 128), axis=1) == text_ids).astype(jnp.float32)
    return (jax.nn.sigmoid(scores) - positive).astype(jnp.bfloat16)


def unpack_rows(ref, rows):
    for k in range(4):
        rows[k * ROWS : (k + 1) * ROWS, :] = ref[k, :ROWS, :]


def id_tile(ids, j):
    return jnp.broadcast_to(ids[:, j * 128 : (j + 1) * 128], (128, 128)).T


def unpack_kernel(text_ref, texts, text_ids):
    unpack_rows(text_ref, texts)
    text_ids[...] = jnp.broadcast_to(id_row(text_ref), text_ids.shape)


def own_kernel(scale_ref, image_ref, texts, text_ids, weights, images, text_sum):
    unpack_rows(image_ref, images)
    text_row = text_ids[0:1, :]
    ids = id_row(image_ref)
    for j in range(GROUP // CHUNK):
        rows = pl.ds(j * CHUNK, CHUNK)
        columns = jnp.concatenate([id_tile(ids, 2 * j), id_tile(ids, 2 * j + 1)], axis=0)
        weights[rows, :] = pair_weights(scale_ref, images[rows, :], texts[...], columns, text_row)
    fold = (((0,), (0,)), ((), ()))
    for j in range(GROUP // CHUNK):
        rows = pl.ds(j * CHUNK, CHUNK)
        text_sum[rows, :] = lax.dot_general(weights[:, rows], images[...], fold, preferred_element_type=jnp.float32)


def other_kernel(scale_ref, image_ref, texts, text_ids, text_sum, image_grads, text_grads, images, weights):
    unpack_rows(image_ref, images)
    factor = scale_ref[0] * 0.125
    text_row = text_ids[0:1, :]
    ids = id_row(image_ref)
    for j in range(GROUP // CHUNK):
        rows = pl.ds(j * CHUNK, CHUNK)
        columns = jnp.concatenate([id_tile(ids, 2 * j), id_tile(ids, 2 * j + 1)], axis=0)
        weight = pair_weights(scale_ref, images[rows, :], texts[...], columns, text_row)
        weights[rows, :] = weight
        grad = jnp.dot(weight, texts[...], preferred_element_type=jnp.float32)
        image_grads[rows, :] = (factor * grad).astype(image_grads.dtype)
    fold = (((0,), (0,)), ((), ()))
    for j in range(GROUP // CHUNK):
        rows = pl.ds(j * CHUNK, CHUNK)
        grad = text_sum[rows, :] + lax.dot_general(weights[:, rows], images[...], fold, preferred_element_type=jnp.float32)
        text_grads[rows, :] = (factor * grad).astype(text_grads.dtype)


def image_shard(scale_ref, shard, weights, texts, received):
    rows = pl.ds(pl.multiple_of(shard * ROWS, ROWS), ROWS)
    grad = jnp.dot(weights[rows, :], texts[...], preferred_element_type=jnp.float32)
    return scale_ref[0] * 0.125 * grad + received[rows, :].astype(jnp.float32)


def image_kernel(scale_ref, place_ref, weights, texts, received, *sent):
    for k, out in zip(STEPS, sent):
        out[...] = image_shard(scale_ref, lax.rem(place_ref[0] + k, 4), weights, texts, received).astype(out.dtype)


def image_sum_kernel(scale_ref, place_ref, weights, texts, received, *rest):
    *parts, out = rest
    total = image_shard(scale_ref, place_ref[0], weights, texts, received)
    for part in parts:
        total = total + part[...].astype(jnp.float32)
    out[...] = total.astype(out.dtype)


def text_sum_kernel(parts, out):
    total = parts[0:ROWS, :].astype(jnp.float32)
    for k in range(1, 4):
        total = total + parts[k * ROWS : (k + 1) * ROWS, :].astype(jnp.float32)
    out[...] = total.astype(out.dtype)


def body(picture_vectors, caption_vectors, picture_match_label, caption_match_label, inverse_softness, score_offset):
    scale = jnp.concatenate([inverse_softness, score_offset])
    place = lax.axis_index("x").astype(jnp.int32).reshape(1)
    packed_images = pack(picture_vectors, picture_match_label)
    packed_texts = pack(caption_vectors, caption_match_label)
    images = lax.ppermute(packed_images, MOVE_AXES, IMAGE_ROUTE)
    texts = lax.ppermute(packed_texts, MOVE_AXES, TEXT_ROUTE)
    own = lax.all_to_all(jnp.broadcast_to(images[None], (4, PACKED, D)), "x", split_axis=0, concat_axis=0, tiled=True)
    other = lax.ppermute(own, "c", [(0, 1), (1, 0)])
    text = lax.all_gather(texts, "y", axis=0)
    half, flops = (GROUP, GROUP), 2 * GROUP * GROUP * D
    rows = (GROUP, D)
    bf16, f32 = jnp.bfloat16, jnp.float32
    all_texts, text_ids = call(unpack_kernel, "unpack_texts", ((rows, bf16), ((8, GROUP), f32)), [VMEM], 40 * flops, text)
    own_weights, _, own_text = call(
        own_kernel, "own_weights", ((half, bf16), (rows, bf16), (rows, f32)), [SMEM, VMEM, VMEM, VMEM], 40 * flops, scale, own, all_texts, text_ids
    )
    other_grad, text_part = call(
        other_kernel, "other_grads", ((rows, bf16), (rows, bf16)), [SMEM] + [VMEM] * 4, 4 * flops, scale, other, all_texts, text_ids, own_text,
        scratch=[pltpu.VMEM(rows, bf16), pltpu.VMEM(half, bf16)],
    )
    received = lax.ppermute(other_grad, "c", [(0, 1), (1, 0)])
    text_parts = lax.all_to_all(text_part, "y", split_axis=0, concat_axis=0, tiled=True)
    shard = ((ROWS, D), bf16)
    sent = call(image_kernel, "image_grads", (shard,) * 3, [SMEM, SMEM] + [VMEM] * 3, 0, scale, place, own_weights, all_texts, received)
    parts = [lax.ppermute(part, "x", [(i, (i + k) % 4) for i in range(4)]) for k, part in zip(STEPS, sent)]
    (kept,) = call(image_sum_kernel, "image_sum", (shard,), [SMEM, SMEM] + [VMEM] * 6, 0, scale, place, own_weights, all_texts, received, *parts)
    image_home = lax.ppermute(kept, MOVE_AXES, back(IMAGE_ROUTE))
    (text_sum,) = call(text_sum_kernel, "text_sum", (shard,), [VMEM], 0, text_parts)
    text_home = lax.ppermute(text_sum, MOVE_AXES, back(TEXT_ROUTE))
    return image_home, text_home.astype(f32)


def solution(mesh):
    fine = Mesh(mesh.devices.reshape(tuple(SIZES.values())), AXES)
    rows, ids = P(AXES, None), P(AXES)
    return jax.shard_map(
        body,
        mesh=fine,
        in_specs=(rows, rows, ids, ids, P(), P()),
        out_specs=(rows, rows),
        check_vma=False,
    )
```
